256 devices in a mesh: snap: 16 (over z, core), vtx: 16 (over y, x).
Axes of the slice: x: 4, y: 4, z: 8, core: 2. Of those that a mesh axis runs over, the one named last changes fastest.
Arguments:
- feats: float32 [16, 16384, 512], P('snap', 'vtx'), may hold values from -6 to 6
- col_ids: int32 [16, 128, 16], P('snap', 'vtx'), may hold values from 0 to 127
- tiles: float32 [16, 128, 16, 128, 128], P('snap', 'vtx'), may hold values from -0.125 to 0.125
- w_first: float32 [512, 256], replicated, may hold values from -0.25 to 0.25
- w_input: float32 [256, 1024], replicated, may hold values from -0.375 to 0.375
- w_recur: float32 [256, 1024], replicated, may hold values from -0.375 to 0.375
- lstm_bias: float32 [1024], replicated, may hold values from -3 to 3
- w_second: float32 [256, 256], replicated, may hold values from -0.375 to 0.375
Outputs:
- output: float32 [16, 16384, 256], P('snap', 'vtx')
The draws below stay inside these ranges and needn't reach their ends.
Inputs may be any that keep to these rules, and one draw needn't show every extreme that they name: `col_ids`: every entry names a row block of the same snapshot's graph; a few blocks are named far more often than others.
All inputs are finite; a program needn't handle non-finite values.
Results may differ from the reference program's by a relative error of at most 0.0003.
Values sent between devices are 32-bit elements; how exact they have to be, the bound alone decides.
A program may use at most 128 MiB of HBM per device.

```python
import math
import jax
import jax.numpy as jnp
import numpy as np
from jax import lax

F = 512
H = 256
TILE = 128
KT = 16
NBLK = 128
VERTS = 16384
SNAPS = 16


def set_ends(entries, stream_key, low, top_value):
    dims = entries.shape
    place = [jax.random.randint(jax.random.fold_in(stream_key, axis), (), 0, dims[axis]) for axis in range(len(dims))]
    entries = entries.at[tuple(place)].set(low)
    longest = dims.index(max(dims))
    place[longest] = (place[longest] + 1) % dims[longest]
    return entries.at[tuple(place)].set(top_value)


def block_scale(key, extent, pieces, least, top_value):
    level, own = 1.0, jax.random.fold_in(key, 6)
    for position, parts in pieces:
        heights = jnp.exp(jax.random.uniform(jax.random.fold_in(own, position), (parts,), jnp.float32, least / len(pieces), top_value / len(pieces)))
        level = level * jnp.repeat(heights, extent[position] // parts).reshape([-1 if axis == position else 1 for axis in range(len(extent))])
    return level


def cumulative_ranks(amount, lean):
    weights = [(1 << 20) // math.isqrt(rank ** lean) + 1 for rank in range(1, amount + 1)]
    scale = 1 + sum(weights) // (1 << 30)
    return np.cumsum(np.array([max(1, weight // scale) for weight in weights]))


def skewed_ids(stream_key, extent, number_of, slope):
    table = cumulative_ranks(number_of, slope)
    lot = jax.random.randint(jax.random.fold_in(stream_key, 1), extent, 0, int(table[number_of - 1]))
    standing = jnp.searchsorted(jnp.asarray(table, jnp.int32), lot, side="right")
    return jax.random.permutation(jax.random.fold_in(stream_key, 2), number_of)[standing].astype(jnp.int32)


def centred(own_key, dims, scale, limit, cuts=(), dtype=jnp.bfloat16):
    factor_of = block_scale(own_key, dims, cuts, -0.22, 0.18) if cuts else 1.0
    entries = jax.random.normal(own_key, dims, jnp.float32) * scale * factor_of
    return jnp.minimum(jnp.maximum(entries, -limit), limit).astype(dtype)


def setup_inputs(seed: int = 0) -> dict:
    keys = jax.random.split(jax.random.key(seed), 9)
    return {
        "feats": centred(keys[0], (SNAPS, VERTS, F), 1.0, 6.0, ((0, 16), (1, 16)), jnp.float32),
        "col_ids": set_ends(skewed_ids(keys[1], (SNAPS, NBLK, KT), NBLK, 2), jax.random.fold_in(keys[1], 3), 0, NBLK - 1).astype(jnp.int32),
        "tiles": centred(keys[2], (SNAPS, NBLK, KT, TILE, TILE), (KT * TILE) ** -0.5, 0.125, ((0, 16), (1, 16)), jnp.float32),
        "w_first": centred(keys[3], (F, H), F ** -0.5, 0.25, (), jnp.float32),
        "w_input": centred(keys[4], (H, 4 * H), H ** -0.5, 0.375, (), jnp.float32),
        "w_recur": centred(keys[5], (H, 4 * H), H ** -0.5, 0.375, (), jnp.float32),
        "lstm_bias": centred(keys[6], (4 * H,), 0.7, 3.0, (), jnp.float32),
        "w_second": centred(keys[7], (H, H), H ** -0.5, 0.375, (), jnp.float32),
    }


def block_sum(tile_set, column_ids, source):
    tile_edge = tile_set.shape[-1]
    width = source.shape[-1]
    blocks = source.reshape(source.shape[0] // tile_edge, tile_edge, width)

    def row_block(operands):
        tiles_here, ids_here = operands
        picked = blocks[ids_here.astype(jnp.int32)]
        return jnp.einsum('ktu,kuw->tw', tiles_here, picked, precision=lax.Precision.HIGHEST)
    summed = lax.map(row_block, (tile_set, column_ids))
    return summed.reshape(-1, width)

def row_scale(tiles):
    sums = lax.optimization_barrier(jnp.sum(tiles * tiles, axis=(2, 4)))
    return lax.rsqrt(1.0 + sums).reshape(tiles.shape[0], -1)[..., None]

def recurrence(pre_time, w_recur, lstm_bias):
    hidden_size = w_recur.shape[0]

    def advance(carry, pre_step):
        state_h, state_c = carry
        gates = pre_step + jnp.dot(state_h, w_recur, precision=lax.Precision.HIGHEST) + lstm_bias
        gate_i = gates[:, :hidden_size]
        gate_f = gates[:, hidden_size:2 * hidden_size]
        gate_g = gates[:, 2 * hidden_size:3 * hidden_size]
        gate_o = gates[:, 3 * hidden_size:]
        state_c = jax.nn.sigmoid(gate_f) * state_c + jax.nn.sigmoid(gate_i) * jnp.tanh(gate_g)
        state_h = jax.nn.sigmoid(gate_o) * jnp.tanh(state_c)
        return ((state_h, state_c), state_h)
    zeros = jnp.zeros((pre_time.shape[1], hidden_size), jnp.float32)
    _, states = lax.scan(advance, (zeros, zeros), pre_time)
    return states

def reference(feats, col_ids, tiles, w_first, w_input, w_recur, lstm_bias, w_second):
    scale = row_scale(tiles)
    mixed = scale * (feats + jax.vmap(block_sum)(tiles, col_ids, feats))
    hidden_one = jax.nn.relu(jnp.einsum('svf,fh->svh', mixed, w_first, precision=lax.Precision.HIGHEST))
    pre = jnp.einsum('svh,hg->svg', hidden_one, w_input, precision=lax.Precision.HIGHEST)
    states = recurrence(pre, w_recur, lstm_bias)
    mixed_two = scale * (states + jax.vmap(block_sum)(tiles, col_ids, states))
    return jnp.einsum('svh,hg->svg', mixed_two, w_second, precision=lax.Precision.HIGHEST)
```

```python
import jax
import jax.numpy as jnp
from jax import lax
from jax.experimental import pallas as pl
from jax.experimental.pallas import tpu as pltpu
from jax.sharding import PartitionSpec as P

BF16, F32 = jnp.bfloat16, jnp.float32


def halves(x):
    high = x.astype(BF16)
    return high, (x - high.astype(F32)).astype(BF16)


def dot(a, b):
    return jnp.dot(a, b, preferred_element_type=F32)


def dot3(a, b_high, b_low):
    a_high, a_low = halves(a)
    return dot(a_high, b_high) + (dot(a_low, b_high) + dot(a_high, b_low))


def conv_kernel(first, ids_ref, tiles_ref, own_ref, whole_ref, out_ref, th, tl, yh, yl):
    row = pl.program_id(0)
    kt, edge = tiles_ref.shape[1], tiles_ref.shape[2]
    squares = jnp.zeros((edge, edge), F32)
    for k in range(kt):
        at = slice(k * edge, (k + 1) * edge)
        tile = tiles_ref[0, k]
        squares += tile * tile
        th[:, at], tl[:, at] = halves(tile)
        yh[at, :], yl[at, :] = halves(whole_ref[ids_ref[row, k]])
    scale = lax.rsqrt(1.0 + jnp.sum(squares, axis=1, keepdims=True))
    total = dot(th[...], yh[...]) + (dot(tl[...], yh[...]) + dot(th[...], yl[...]))
    total = scale * (own_ref[...] + total)
    out_ref[...] = jnp.maximum(total, 0.0) if first else total


def conv(first, tiles, ids, own, whole):
    blocks, kt, edge, _ = tiles.shape
    width = own.shape[-1]
    return pl.pallas_call(
        lambda *refs: conv_kernel(first, *refs),
        grid=(blocks,),
        in_specs=[
            pl.BlockSpec(memory_space=pltpu.SMEM),
            pl.BlockSpec((1, kt, edge, edge), lambda r: (r, 0, 0, 0)),
            pl.BlockSpec((edge, width), lambda r: (r, 0)),
            pl.BlockSpec(memory_space=pltpu.VMEM),
        ],
        out_specs=pl.BlockSpec((edge, width), lambda r: (r, 0)),
        out_shape=jax.ShapeDtypeStruct(own.shape, F32),
        scratch_shapes=[
            pltpu.VMEM((edge, kt * edge), BF16),
            pltpu.VMEM((edge, kt * edge), BF16),
            pltpu.VMEM((kt * edge, width), BF16),
            pltpu.VMEM((kt * edge, width), BF16),
        ],
        compiler_params=pltpu.CompilerParams(vmem_limit_bytes=44 << 20),
    )(ids, tiles, own, whole)


def sigmoid(x):
    return 0.5 * jnp.tanh(0.5 * x) + 0.5


def lstm_kernel(x_ref, w_in_ref, w_rec_ref, bias_ref, w_two_ref, out_ref, pre, wh, wl, rh, rl):
    steps, rows, hidden = x_ref.shape
    wh[...], wl[...] = halves(w_in_ref[...])
    rh[...], rl[...] = halves(w_rec_ref[...])

    def fill(s, _):
        pre[s] = dot3(x_ref[s], wh[...], wl[...]) + bias_ref[...]
        return 0

    lax.fori_loop(0, steps, fill, 0)

    def advance(s, carry):
        h, c = carry
        gates = pre[s] + dot3(h, rh[...], rl[...])
        i, f, g, o = (gates[:, q * hidden : (q + 1) * hidden] for q in range(4))
        c = sigmoid(f) * c + sigmoid(i) * jnp.tanh(g)
        h = sigmoid(o) * jnp.tanh(c)
        out_ref[s] = h
        return h, c

    zeros = jnp.zeros((rows, hidden), F32)
    lax.fori_loop(0, steps, advance, (zeros, zeros))
    two_high, two_low = halves(w_two_ref[...])
    states = out_ref[...].reshape(steps * rows, hidden)
    out_ref[...] = dot3(states, two_high, two_low).reshape(steps, rows, hidden)


def lstm(x, w_input, w_recur, bias, w_second):
    steps, rows, hidden = x.shape
    return pl.pallas_call(
        lstm_kernel,
        in_specs=[pl.BlockSpec(memory_space=pltpu.VMEM)] * 5,
        out_specs=pl.BlockSpec(memory_space=pltpu.VMEM),
        out_shape=jax.ShapeDtypeStruct(x.shape, F32),
        scratch_shapes=[
            pltpu.VMEM((steps, rows, 4 * hidden), F32),
            pltpu.VMEM((hidden, 4 * hidden), BF16),
            pltpu.VMEM((hidden, 4 * hidden), BF16),
            pltpu.VMEM((hidden, 4 * hidden), BF16),
            pltpu.VMEM((hidden, 4 * hidden), BF16),
        ],
        compiler_params=pltpu.CompilerParams(vmem_limit_bytes=40 << 20),
    )(x, w_input, w_recur, bias.reshape(1, -1), w_second)


def on_device(feats, col_ids, tiles, w_first, w_input, w_recur, lstm_bias, w_second):
    feats, ids, tiles = feats[0], col_ids[0], tiles[0]
    edge, hidden = tiles.shape[-1], w_second.shape[0]
    y = jnp.dot(feats, w_first, precision=lax.Precision.HIGH)
    whole = lax.all_gather(y, "vtx", axis=0, tiled=True).reshape(-1, edge, hidden)
    hidden_one = conv(True, tiles, ids, y, whole)
    timelines = lax.all_to_all(hidden_one[None], "snap", split_axis=1, concat_axis=0, tiled=True)
    states = lstm(timelines, w_input, w_recur, lstm_bias, w_second)
    z = lax.all_to_all(states, "snap", split_axis=0, concat_axis=1, tiled=True)[0]
    whole = lax.all_gather(z, "vtx", axis=0, tiled=True).reshape(-1, edge, hidden)
    return conv(False, tiles, ids, z, whole)[None]


def solution(mesh):
    placed = (
        P("snap", "vtx", None),
        P("snap", "vtx", None),
        P("snap", "vtx", None, None, None),
        P(),
        P(),
        P(),
        P(),
        P(),
    )
    return jax.shard_map(
        on_device, mesh=mesh, in_specs=placed, out_specs=P("snap", "vtx", None), check_vma=False
    )
```

```python
import jax
import jax.numpy as jnp
from jax import lax
from jax.experimental import pallas as pl
from jax.experimental.pallas import tpu as pltpu
from jax.sharding import PartitionSpec as P

BF16, F32 = jnp.bfloat16, jnp.float32
MESH = pl.DeviceIdType.MESH
SIDE = 4
SNAPS = 16
EDGE = 128
LANES = 128
KT = 16
BLOCKS = 8
BATCH = 32
HIDDEN = 256
GATHER_SEMS = 40


def halves(x):
    high = x.astype(BF16)
    return high, (x - high.astype(F32)).astype(BF16)


def dot(a, b):
    return jnp.dot(a, b, preferred_element_type=F32)


def dot3(a, b_high, b_low):
    a_high, a_low = halves(a)
    return dot(a_high, b_high) + (dot(a_low, b_high) + dot(a_high, b_low))


def sigmoid(x):
    return 0.5 * jnp.tanh(0.5 * x) + 0.5


class Gather:
    def __init__(self, buffer, source, first, count, send_sem, recv_sem, base):
        self.buffer, self.source, self.first, self.count = buffer, source, first, count
        self.send_sem, self.recv_sem, self.base = send_sem, recv_sem, base
        me = lax.axis_index("vtx")
        self.x, self.y = lax.rem(me, SIDE), lax.div(me, SIDE)
        self.me = me
        self.started = []

    def device(self, half, da, db):
        dx, dy = (da, db) if half == 0 else (db, da)
        return lax.rem(self.y + (dy + SIDE), SIDE) * SIDE + lax.rem(self.x + (dx + SIDE), SIDE)

    def rows(self, half, part):
        size = self.count // 2
        start = half * size
        if part is not None:
            size //= 2
            start += part * size
        return start, size

    def place(self, half, da, db, part):
        start, size = self.rows(half, part)
        return self.buffer.at[pl.ds(self.device(half, da, db) * BLOCKS + (self.first + start), size)]

    def number(self, half, da, db, part):
        along = {-1: 0, 1: 1, 2: 2}
        if db == 0:
            number = along[da]
            number += part or 0
        else:
            number = 4 + 4 * (0, -1, 1, 2).index(da) + along[db] + (part or 0)
        return self.base + half * 20 + number

    def copy(self, half, axis, way, da, db, part):
        seen = lambda d: 2 if d in (-1, 1) and d == -way else -way
        if axis == 0:
            to, number = self.device(half, way, 0), self.number(half, seen(da), db, part)
        else:
            to, number = self.device(half, 0, way), self.number(half, da, seen(db), part)
        place = self.place(half, da, db, part)
        source = place
        if da == 0 and db == 0 and self.source is not None:
            start, size = self.rows(half, part)
            source = self.source.at[pl.ds(self.first + start, size)]
        return pltpu.make_async_remote_copy(
            src_ref=source,
            dst_ref=place,
            send_sem=self.send_sem.at[number],
            recv_sem=self.recv_sem.at[number],
            device_id={"vtx": to},
            device_id_type=MESH,
        )

    def send(self, half, axis, way, da, db, part=None):
        copy = self.copy(half, axis, way, da, db, part)
        copy.start()
        self.started.append(copy)

    def wait(self, half, da, db, part=None):
        number = self.number(half, da, db, part)
        place = self.place(half, da, db, part)
        pltpu.make_async_remote_copy(
            src_ref=place,
            dst_ref=place,
            send_sem=self.send_sem.at[number],
            recv_sem=self.recv_sem.at[number],
            device_id={"vtx": self.device(half, 1, 0)},
            device_id_type=MESH,
        ).wait_recv()

    def both(self, half, da):
        for way in (1, -1):
            self.send(half, 1, way, da, 0)

    def own(self):
        for half in (0, 1):
            for way in (1, -1):
                self.send(half, 0, way, 0, 0)
        for half in (0, 1):
            self.both(half, 0)

    def ring(self):
        for half in (0, 1):
            self.wait(half, -1, 0)
            self.send(half, 0, 1, -1, 0, 0)
            self.wait(half, 1, 0)
            self.send(half, 0, -1, 1, 0, 1)
        for half in (0, 1):
            self.both(half, -1)
            self.both(half, 1)

    def onward(self, da):
        for half in (0, 1):
            self.wait(half, da, -1)
            self.send(half, 1, 1, da, -1, 0)
            self.wait(half, da, 1)
            self.send(half, 1, -1, da, 1, 1)

    def opposite(self):
        for half in (0, 1):
            self.wait(half, 2, 0, 0)
            self.wait(half, 2, 0, 1)
            self.both(half, 2)

    def last(self):
        for da in (0, -1, 1, 2):
            for half in (0, 1):
                for part in (0, 1):
                    self.wait(half, da, 2, part)

    def wait_sent(self):
        for copy in self.started:
            copy.wait_send()


def kernel(
    ids_ref, feats_ref, w_first_ref, bias_ref, tiles_hbm, w_in_hbm, w_rec_hbm, w_two_hbm, out_ref,
    buf0, buf1, staged, tcat, scales, ycat, hid, xin, pre, zout, zin,
    w_in, w_rec, w_two, in_high, in_low, rec_high, rec_low,
    g_send, g_recv, x_send, x_recv, z_send, z_recv, local_sem, tile_sem, weight_sem, free_sem,
):
    snap, me = lax.axis_index("snap"), lax.axis_index("vtx")
    x, y = lax.rem(me, SIDE), lax.div(me, SIDE)
    bufs = (buf0, buf1)
    others = [lax.rem(snap + k, SNAPS) for k in range(1, SNAPS)]
    beside = [
        lax.rem(y + dy, SIDE) * SIDE + lax.rem(x + dx, SIDE)
        for dx, dy in ((1, 0), (SIDE - 1, 0), (0, 1), (0, SIDE - 1))
    ]

    weights = [
        pltpu.make_async_copy(a, b, weight_sem.at[i])
        for i, (a, b) in enumerate(((w_in_hbm, w_in), (w_rec_hbm, w_rec), (w_two_hbm, w_two)))
    ]

    def tile_copy(r):
        return pltpu.make_async_copy(tiles_hbm.at[r], staged.at[r], tile_sem.at[r])

    barrier = pltpu.get_barrier_semaphore()
    for device in beside:
        pl.semaphore_signal(barrier, inc=1, device_id={"vtx": device}, device_id_type=MESH)
    for device in others:
        pl.semaphore_signal(barrier, inc=1, device_id={"snap": device}, device_id_type=MESH)

    for r in range(BLOCKS):
        tile_copy(r).start()
    for copy in weights:
        copy.start()

    def first_product(c):
        high, low = halves(w_first_ref[:, c * LANES : (c + 1) * LANES])

        def some(i, _):
            part = dot3(feats_ref[pl.ds(i * 256, 256), :], high, low)
            bufs[c][me * BLOCKS + 2 * i] = part[:EDGE]
            bufs[c][me * BLOCKS + 2 * i + 1] = part[EDGE:]
            return 0

        lax.fori_loop(0, BLOCKS // 2, some, 0)

    first_product(0)
    pl.semaphore_wait(barrier, len(beside) + len(others))

    one = [Gather(bufs[c], None, 0, BLOCKS, g_send, g_recv, c * GATHER_SEMS) for c in (0, 1)]
    one[0].own()
    first_product(1)

    def split_tiles(start, stop):
        def block(r, _):
            tile_copy(r).wait()
            squares = jnp.zeros((EDGE, EDGE), F32)
            for k in range(KT):
                tile = staged[r, k]
                squares += tile * tile
                high, low = halves(tile)
                tcat[r, :EDGE, k * EDGE : (k + 1) * EDGE] = high
                tcat[r, EDGE:, k * EDGE : (k + 1) * EDGE] = low
            scale = lax.rsqrt(1.0 + jnp.sum(squares, axis=1, keepdims=True))
            scales[r] = jnp.broadcast_to(scale, (EDGE, LANES))
            return 0

        lax.fori_loop(start, stop, block, 0)

    def conv(c, start, stop, first):
        def block(r, _):
            for k in range(KT):
                high, low = halves(bufs[c][ids_ref[r, k]])
                ycat[k * EDGE : (k + 1) * EDGE, :LANES] = high
                ycat[k * EDGE : (k + 1) * EDGE, LANES:] = low
            out = dot(tcat[r], ycat[...])
            total = (out[:EDGE, :LANES] + out[:EDGE, LANES:]) + (out[EDGE:, :LANES] + out[EDGE:, LANES:])
            total = scales[r] * (bufs[c][me * BLOCKS + r] + total)
            if first:
                hid[c, r] = jnp.maximum(total, 0.0)
            else:
                out_ref[pl.ds(pl.multiple_of(r * EDGE, EDGE), EDGE), c * LANES : (c + 1) * LANES] = total
            return 0

        lax.fori_loop(start, stop, block, 0)

    def shares(ref, c, b, j):
        rows = pl.ds(pl.multiple_of(lax.rem(j, 4) * BATCH, BATCH), BATCH)
        return ref.at[c, 4 * b + lax.div(j, 4), rows]

    x_sent = []

    def x_copy(c, b, k):
        to = others[k - 1]
        return pltpu.make_async_remote_copy(
            src_ref=shares(hid, c, b, to),
            dst_ref=xin.at[c, b, snap],
            send_sem=x_send.at[c, b, k],
            recv_sem=x_recv.at[c, b, k],
            device_id={"snap": to},
            device_id_type=MESH,
        )

    def x_local(c, b):
        return pltpu.make_async_copy(shares(hid, c, b, snap), xin.at[c, b, snap], x_send.at[c, b, 0])

    def x_start(c, b):
        for k in range(1, SNAPS):
            copy = x_copy(c, b, k)
            copy.start()
            x_sent.append(copy)
        x_local(c, b).start()

    def x_wait(c, b):
        x_local(c, b).wait()
        for k in range(1, SNAPS):
            source = lax.rem(snap + (SNAPS - k), SNAPS)
            pltpu.make_async_remote_copy(
                src_ref=xin.at[c, b, source],
                dst_ref=xin.at[c, b, source],
                send_sem=x_send.at[c, b, k],
                recv_sem=x_recv.at[c, b, k],
                device_id={"snap": source},
                device_id_type=MESH,
            ).wait_recv()

    def input_product(c, b):
        deep = slice(c * LANES, (c + 1) * LANES)

        def some(i, _):
            rows = pl.ds(pl.multiple_of(i * EDGE, EDGE), EDGE)
            part = dot3(xin[c, b, pl.ds(i * 4, 4)].reshape(EDGE, LANES), in_high[deep, :], in_low[deep, :])
            pre[b, rows] = part + (bias_ref[...] if c == 0 else pre[b, rows])
            return 0

        lax.fori_loop(0, SNAPS * BATCH // EDGE, some, 0)

    def z_copy(b, s):
        return pltpu.make_async_remote_copy(
            src_ref=zout.at[b, s],
            dst_ref=shares(zin, slice(None), b, snap),
            send_sem=z_send.at[b, s],
            recv_sem=z_recv.at[b, snap],
            device_id={"snap": s},
            device_id_type=MESH,
        )

    def z_local(b):
        return pltpu.make_async_copy(zout.at[b, snap], shares(zin, slice(None), b, snap), local_sem.at[b])

    def z_start(b, s, z):
        zout[b, s, 0] = z[:, :LANES]
        zout[b, s, 1] = z[:, LANES:]

        @pl.when(s != snap)
        def _():
            z_copy(b, s).start()

        @pl.when(s == snap)
        def _():
            z_local(b).start()

    def z_wait(b):
        z_local(b).wait()
        for source in others:
            pltpu.make_async_remote_copy(
                src_ref=shares(zin, slice(None), b, source),
                dst_ref=shares(zin, slice(None), b, source),
                send_sem=z_send.at[b, source],
                recv_sem=z_recv.at[b, source],
                device_id={"snap": source},
                device_id_type=MESH,
            ).wait_recv()
        for c in (0, 1):
            for i in range(4 * b, 4 * b + 4):
                bufs[c][me * BLOCKS + i] = zin[c, i]

    def cell(gates, state_c):
        i, f, g, o = (gates[:, q * HIDDEN : (q + 1) * HIDDEN] for q in range(4))
        state_c = sigmoid(f) * state_c + sigmoid(i) * jnp.tanh(g)
        return sigmoid(o) * jnp.tanh(state_c), state_c

    def begin(b):
        return cell(pre[b, :BATCH], jnp.zeros((BATCH, HIDDEN), F32))

    def product(h):
        high, low = halves(h)
        both = dot(jnp.concatenate([high, low], axis=0), rec_high[...])
        return both[:BATCH] + (both[BATCH:] + dot(high, rec_low[...]))

    def steps(b, start, stop, carry):
        def advance(s, carry):
            h, state_c = carry
            wide = product(h)
            rows = pl.ds(pl.multiple_of(s * BATCH, BATCH), BATCH)
            new = cell(pre[b, rows] + wide[:, : 4 * HIDDEN], state_c)
            z_start(b, s - 1, wide[:, 4 * HIDDEN :])
            return new

        return lax.fori_loop(start, stop, advance, carry)

    def finish(b, carry):
        last = slice(4 * HIDDEN, 5 * HIDDEN)
        z_start(b, SNAPS - 1, dot3(carry[0], rec_high[:, last], rec_low[:, last]))

    split_tiles(0, 4)
    one[0].ring()
    split_tiles(4, 8)
    for copy in weights:
        copy.wait()
    in_high[...], in_low[...] = halves(w_in[...])
    rec_high[:, : 4 * HIDDEN], rec_low[:, : 4 * HIDDEN] = halves(w_rec[...])
    rec_high[:, 4 * HIDDEN :], rec_low[:, 4 * HIDDEN :] = halves(w_two[...])
    one[0].onward(0)
    one[0].opposite()
    one[0].onward(-1)
    one[0].onward(1)
    one[1].own()
    one[0].onward(2)
    one[0].last()

    conv(0, 0, 4, True)
    x_start(0, 0)
    one[1].ring()
    conv(0, 4, 8, True)
    x_start(0, 1)
    one[1].onward(0)
    one[1].opposite()
    x_wait(0, 0)
    x_wait(0, 1)
    input_product(0, 0)
    one[1].onward(-1)
    one[1].onward(1)
    input_product(0, 1)
    one[1].onward(2)
    one[1].last()

    conv(1, 0, 4, True)
    x_start(1, 0)
    conv(1, 4, 8, True)
    x_start(1, 1)
    one[0].wait_sent()
    one[1].wait_sent()
    for device in beside:
        pl.semaphore_signal(free_sem, inc=1, device_id={"vtx": device}, device_id_type=MESH)

    x_wait(1, 0)
    input_product(1, 0)
    finish(0, steps(0, 1, SNAPS, begin(0)))
    x_wait(1, 1)
    input_product(1, 1)
    carry = steps(1, 1, 8, begin(1))
    z_wait(0)
    pl.semaphore_wait(free_sem, len(beside))
    two = [
        [
            Gather(bufs[c], zin.at[c], 4 * b, 4, g_send, g_recv, (2 + 2 * b + c) * GATHER_SEMS)
            for c in (0, 1)
        ]
        for b in (0, 1)
    ]
    two[0][0].own()
    two[0][1].own()
    finish(1, steps(1, 8, SNAPS, carry))
    two[0][0].ring()
    two[0][1].ring()
    z_wait(1)
    two[1][0].own()
    two[0][0].onward(0)
    two[0][0].opposite()
    two[0][1].onward(0)
    two[0][1].opposite()
    for da in (-1, 1, 2):
        two[0][0].onward(da)
    two[1][1].own()
    two[1][0].ring()
    for da in (-1, 1, 2):
        two[0][1].onward(da)
    two[1][0].onward(0)
    two[1][0].opposite()
    two[1][1].ring()
    for da in (-1, 1, 2):
        two[1][0].onward(da)
    two[0][0].last()
    two[0][1].last()
    two[1][0].last()
    conv(0, 0, 2, False)
    two[1][1].onward(0)
    two[1][1].opposite()
    conv(0, 2, 4, False)
    two[1][1].onward(-1)
    two[1][1].onward(1)
    conv(0, 4, 8, False)
    two[1][1].onward(2)
    two[1][1].last()
    conv(1, 0, 8, False)

    for b in (0, 1):
        for c in (0, 1):
            two[b][c].wait_sent()
    for copy in x_sent:
        copy.wait_send()
    for b in (0, 1):
        for device in others:
            z_copy(b, device).wait_send()


def on_device(feats, col_ids, tiles, w_first, w_input, w_recur, lstm_bias, w_second):
    rows = BLOCKS * EDGE
    whole = (lax.axis_size("vtx") * BLOCKS, EDGE, LANES)
    vmem, hbm = pl.BlockSpec(memory_space=pltpu.VMEM), pl.BlockSpec(memory_space=pl.ANY)
    dma = pltpu.SemaphoreType.DMA
    out = pl.pallas_call(
        kernel,
        in_specs=[pl.BlockSpec(memory_space=pltpu.SMEM), vmem, vmem, vmem, hbm, hbm, hbm, hbm],
        out_specs=vmem,
        out_shape=jax.ShapeDtypeStruct((rows, HIDDEN), F32),
        scratch_shapes=[
            pltpu.VMEM(whole, F32),
            pltpu.VMEM(whole, F32),
            pltpu.VMEM((BLOCKS, KT, EDGE, EDGE), F32),
            pltpu.VMEM((BLOCKS, 2 * EDGE, KT * EDGE), BF16),
            pltpu.VMEM((BLOCKS, EDGE, LANES), F32),
            pltpu.VMEM((KT * EDGE, 2 * LANES), BF16),
            pltpu.VMEM((2, BLOCKS, EDGE, LANES), F32),
            pltpu.VMEM((2, 2, SNAPS, BATCH, LANES), F32),
            pltpu.VMEM((2, SNAPS * BATCH, 4 * HIDDEN), F32),
            pltpu.VMEM((2, SNAPS, 2, BATCH, LANES), F32),
            pltpu.VMEM((2, BLOCKS, EDGE, LANES), F32),
            pltpu.VMEM((HIDDEN, 4 * HIDDEN), F32),
            pltpu.VMEM((HIDDEN, 4 * HIDDEN), F32),
            pltpu.VMEM((HIDDEN, HIDDEN), F32),
            pltpu.VMEM((HIDDEN, 4 * HIDDEN), BF16),
            pltpu.VMEM((HIDDEN, 4 * HIDDEN), BF16),
            pltpu.VMEM((HIDDEN, 5 * HIDDEN), BF16),
            pltpu.VMEM((HIDDEN, 5 * HIDDEN), BF16),
            dma((6 * GATHER_SEMS,)),
            dma((6 * GATHER_SEMS,)),
            dma((2, 2, SNAPS)),
            dma((2, 2, SNAPS)),
            dma((2, SNAPS)),
            dma((2, SNAPS)),
            dma((2,)),
            dma((BLOCKS,)),
            dma((3,)),
            pltpu.SemaphoreType.REGULAR,
        ],
        compiler_params=pltpu.CompilerParams(
            collective_id=0, has_side_effects=True, vmem_limit_bytes=58 << 20
        ),
    )(
        col_ids[0], feats[0], w_first, lstm_bias.reshape(1, -1), tiles[0], w_input, w_recur, w_second
    )
    return out[None]


def solution(mesh):
    placed = (
        P("snap", "vtx", None),
        P("snap", "vtx", None),
        P("snap", "vtx", None, None, None),
        P(),
        P(),
        P(),
        P(),
        P(),
    )
    return jax.shard_map(
        on_device, mesh=mesh, in_specs=placed, out_specs=P("snap", "vtx", None), check_vma=False
    )
```

```python
import jax
import jax.numpy as jnp
from jax import lax
from jax.experimental import pallas as pl
from jax.experimental.pallas import tpu as pltpu
from jax.sharding import PartitionSpec as P

BF16, F32 = jnp.bfloat16, jnp.float32
MESH = pl.DeviceIdType.MESH
SIDE = 4
SNAPS = 16
EDGE = 128
LANES = 128
KT = 16
BLOCKS = 8
BATCHES = (16, 48)
ROWS = 1024
EARLY = SNAPS * BATCHES[0] // EDGE
HIDDEN = 256
GATHER_SEMS = 40


def halves(x):
    high = x.astype(BF16)
    return high, (x - high.astype(F32)).astype(BF16)


def dot(a, b):
    return jnp.dot(a, b, preferred_element_type=F32)


def dot3(a, b_high, b_low):
    a_high, a_low = halves(a)
    return dot(a_high, b_high) + (dot(a_low, b_high) + dot(a_high, b_low))


def sigmoid(x):
    return 0.5 * jnp.tanh(0.5 * x) + 0.5


class Gather:
    def __init__(self, buffer, first, count, send_sem, recv_sem, base):
        self.buffer, self.first, self.count = buffer, first, count
        self.send_sem, self.recv_sem, self.base = send_sem, recv_sem, base
        me = lax.axis_index("vtx")
        self.x, self.y = lax.rem(me, SIDE), lax.div(me, SIDE)
        self.me = me
        self.started = []

    def device(self, half, da, db):
        dx, dy = (da, db) if half == 0 else (db, da)
        return lax.rem(self.y + (dy + SIDE), SIDE) * SIDE + lax.rem(self.x + (dx + SIDE), SIDE)

    def place(self, half, da, db, part):
        size = self.count // 2
        block = self.device(half, da, db) * BLOCKS + (self.first + half * size)
        if part is None:
            return self.buffer.at[pl.ds(block, size)]
        if size == 1:
            return self.buffer.at[pl.ds(block, 1), pl.ds(part * (EDGE // 2), EDGE // 2)]
        longer_last = half == 1 if db == 0 else da in (-1, 1)
        cut = size // 2 if longer_last else size - size // 2
        return self.buffer.at[pl.ds(block + part * cut, size - cut if part else cut)]

    def number(self, half, da, db, part):
        along = {-1: 0, 1: 1, 2: 2}
        if db == 0:
            number = along[da]
            number += part or 0
        else:
            number = 4 + 4 * (0, -1, 1, 2).index(da) + along[db] + (part or 0)
        return self.base + half * 20 + number

    def copy(self, half, axis, way, da, db, part):
        seen = lambda d: 2 if d in (-1, 1) and d == -way else -way
        if axis == 0:
            to, number = self.device(half, way, 0), self.number(half, seen(da), db, part)
        else:
            to, number = self.device(half, 0, way), self.number(half, da, seen(db), part)
        place = self.place(half, da, db, part)
        return pltpu.make_async_remote_copy(
            src_ref=place,
            dst_ref=place,
            send_sem=self.send_sem.at[number],
            recv_sem=self.recv_sem.at[number],
            device_id={"vtx": to},
            device_id_type=MESH,
        )

    def send(self, half, axis, way, da, db, part=None):
        copy = self.copy(half, axis, way, da, db, part)
        copy.start()
        self.started.append(copy)

    def wait(self, half, da, db, part=None):
        number = self.number(half, da, db, part)
        place = self.place(half, da, db, part)
        pltpu.make_async_remote_copy(
            src_ref=place,
            dst_ref=place,
            send_sem=self.send_sem.at[number],
            recv_sem=self.recv_sem.at[number],
            device_id={"vtx": self.device(half, 1, 0)},
            device_id_type=MESH,
        ).wait_recv()

    def both(self, half, da):
        for way in (1, -1):
            self.send(half, 1, way, da, 0)

    def own_half(self, half):
        for way in (1, -1):
            self.send(half, 0, way, 0, 0)
        self.both(half, 0)

    def own(self):
        for half in (0, 1):
            for way in (1, -1):
                self.send(half, 0, way, 0, 0)
        for half in (0, 1):
            self.both(half, 0)

    def ring(self):
        for half in (0, 1):
            self.wait(half, -1, 0)
            self.send(half, 0, 1, -1, 0, 0)
            self.wait(half, 1, 0)
            self.send(half, 0, -1, 1, 0, 1)
        for half in (0, 1):
            self.both(half, -1)
            self.both(half, 1)

    def onward(self, da):
        for half in (0, 1):
            self.wait(half, da, -1)
            self.send(half, 1, 1, da, -1, 0)
            self.wait(half, da, 1)
            self.send(half, 1, -1, da, 1, 1)

    def opposite(self):
        for half in (0, 1):
            self.wait(half, 2, 0, 0)
            self.wait(half, 2, 0, 1)
            self.both(half, 2)

    def last(self):
        for da in (0, -1, 1, 2):
            for half in (0, 1):
                for part in (0, 1):
                    self.wait(half, da, 2, part)

    def wait_sent(self):
        for copy in self.started:
            copy.wait_send()


def kernel(
    ids_ref, bias_ref, feats_hbm, w_first_hbm, tiles_hbm, w_in_hbm, w_rec_hbm, w_two_hbm, out_ref,
    buf0, buf1, staged, tcat, scales, ycat, hid, xin0, xin1, pre0, pre1, zout0, zout1, zin,
    feats, w_first, w_in, w_rec, w_two, in_high, in_low, rec_high, rec_low,
    g_send, g_recv, x_send, x_recv, z_send, z_recv, local_sem, tile_sem, feats_sem, weight_sem, free_sem,
):
    snap, me = lax.axis_index("snap"), lax.axis_index("vtx")
    x, y = lax.rem(me, SIDE), lax.div(me, SIDE)
    bufs, xin, pre, zout = (buf0, buf1), (xin0, xin1), (pre0, pre1), (zout0, zout1)
    firsts = (0, SNAPS * BATCHES[0])
    others = [lax.rem(snap + k, SNAPS) for k in range(1, SNAPS)]
    beside = [
        lax.rem(y + dy, SIDE) * SIDE + lax.rem(x + dx, SIDE)
        for dx, dy in ((1, 0), (SIDE - 1, 0), (0, 1), (0, SIDE - 1))
    ]

    weights = [
        pltpu.make_async_copy(a, b, weight_sem.at[i])
        for i, (a, b) in enumerate(((w_in_hbm, w_in), (w_rec_hbm, w_rec), (w_two_hbm, w_two)))
    ]
    first_copies = [
        pltpu.make_async_copy(w_first_hbm.at[rows], w_first.at[rows], feats_sem.at[BLOCKS + i])
        for i, rows in enumerate((slice(0, HIDDEN), slice(HIDDEN, 2 * HIDDEN)))
    ]
    feats_copies = [
        pltpu.make_async_copy(feats_hbm.at[rows], feats.at[rows], feats_sem.at[r])
        for r, rows in enumerate(slice(r * EDGE, (r + 1) * EDGE) for r in range(BLOCKS))
    ]

    def tile_copy(r):
        return pltpu.make_async_copy(tiles_hbm.at[r], staged.at[r], tile_sem.at[r])

    for copy in (*first_copies, *feats_copies):
        copy.start()
    barrier = pltpu.get_barrier_semaphore()
    for device in beside:
        pl.semaphore_signal(barrier, inc=1, device_id={"vtx": device}, device_id_type=MESH)
    for device in others:
        pl.semaphore_signal(barrier, inc=1, device_id={"snap": device}, device_id_type=MESH)

    one = [Gather(bufs[c], 0, BLOCKS, g_send, g_recv, c * GATHER_SEMS) for c in (0, 1)]
    for copy in first_copies:
        copy.wait()

    def first_product(c, half):
        high, low = halves(w_first[:, c * LANES : (c + 1) * LANES])
        for r in range(4 * half, 4 * half + 4):
            if c == 0:
                feats_copies[r].wait()
            bufs[c][me * BLOCKS + r] = dot3(feats[r * EDGE : (r + 1) * EDGE, :], high, low)

    first_product(0, 0)
    pl.semaphore_wait(barrier, len(beside) + len(others))
    one[0].own_half(0)
    first_product(0, 1)
    one[0].own_half(1)
    for r in range(BLOCKS):
        tile_copy(r).start()
    for copy in weights:
        copy.start()
    first_product(1, 0)
    first_product(1, 1)

    def split_tiles(start, stop):
        def block(r, _):
            tile_copy(r).wait()
            squares = jnp.zeros((EDGE, EDGE), F32)
            for k in range(KT):
                tile = staged[r, k]
                squares += tile * tile
                high, low = halves(tile)
                tcat[r, :EDGE, k * EDGE : (k + 1) * EDGE] = high
                tcat[r, EDGE:, k * EDGE : (k + 1) * EDGE] = low
            scale = lax.rsqrt(1.0 + jnp.sum(squares, axis=1, keepdims=True))
            scales[r] = jnp.broadcast_to(scale, (EDGE, LANES))
            return 0

        lax.fori_loop(start, stop, block, 0)

    def conv(c, start, stop, first):
        def block(r, _):
            for k in range(KT):
                high, low = halves(bufs[c][ids_ref[r, k]])
                ycat[k * EDGE : (k + 1) * EDGE, :LANES] = high
                ycat[k * EDGE : (k + 1) * EDGE, LANES:] = low
            out = dot(tcat[r], ycat[...])
            total = (out[:EDGE, :LANES] + out[:EDGE, LANES:]) + (out[EDGE:, :LANES] + out[EDGE:, LANES:])
            rows = pl.ds(pl.multiple_of(r * EDGE, EDGE), EDGE)
            total = scales[r] * (bufs[c][me * BLOCKS + r] + total)
            if first:
                hid[c, rows] = jnp.maximum(total, 0.0)
            else:
                out_ref[rows, c * LANES : (c + 1) * LANES] = total
            return 0

        lax.fori_loop(start, stop, block, 0)

    def shares(ref, c, b, j):
        return ref.at[c, pl.ds(pl.multiple_of(firsts[b] + j * BATCHES[b], 16), BATCHES[b])]

    x_sent = []

    def x_copy(c, b, k):
        to = others[k - 1]
        return pltpu.make_async_remote_copy(
            src_ref=shares(hid, c, b, to),
            dst_ref=xin[b].at[c, snap],
            send_sem=x_send.at[c, b, k],
            recv_sem=x_recv.at[c, b, k],
            device_id={"snap": to},
            device_id_type=MESH,
        )

    def x_local(c, b):
        return pltpu.make_async_copy(shares(hid, c, b, snap), xin[b].at[c, snap], x_send.at[c, b, 0])

    def x_start(c, b):
        for k in range(1, SNAPS):
            copy = x_copy(c, b, k)
            copy.start()
            x_sent.append(copy)
        x_local(c, b).start()

    def x_wait(c, b):
        x_local(c, b).wait()
        for k in range(1, SNAPS):
            source = lax.rem(snap + (SNAPS - k), SNAPS)
            pltpu.make_async_remote_copy(
                src_ref=xin[b].at[c, source],
                dst_ref=xin[b].at[c, source],
                send_sem=x_send.at[c, b, k],
                recv_sem=x_recv.at[c, b, k],
                device_id={"snap": source},
                device_id_type=MESH,
            ).wait_recv()

    def input_product(b):
        count = 256 // BATCHES[b] if b == 0 else 4
        size = count * BATCHES[b]

        def some(i, _):
            rows = pl.ds(pl.multiple_of(i * size, size), size)
            steps = pl.ds(i * count, count)
            both = [xin[b][c, steps].reshape(size, LANES) for c in (0, 1)]
            pre[b][rows] = dot3(jnp.concatenate(both, axis=1), in_high[...], in_low[...]) + bias_ref[...]
            return 0

        lax.fori_loop(0, SNAPS // count, some, 0)

    def z_copy(b, s):
        return pltpu.make_async_remote_copy(
            src_ref=zout[b].at[s],
            dst_ref=shares(zin, slice(None), b, snap),
            send_sem=z_send.at[b, s],
            recv_sem=z_recv.at[b, snap],
            device_id={"snap": s},
            device_id_type=MESH,
        )

    def z_local(b):
        return pltpu.make_async_copy(zout[b].at[snap], shares(zin, slice(None), b, snap), local_sem.at[b])

    def z_start(b, s, z):
        zout[b][s, 0] = z[:, :LANES]
        zout[b][s, 1] = z[:, LANES:]

        @pl.when(s != snap)
        def _():
            z_copy(b, s).start()

        @pl.when(s == snap)
        def _():
            z_local(b).start()

    def z_wait(b):
        z_local(b).wait()
        for source in others:
            pltpu.make_async_remote_copy(
                src_ref=shares(zin, slice(None), b, source),
                dst_ref=shares(zin, slice(None), b, source),
                send_sem=z_send.at[b, source],
                recv_sem=z_recv.at[b, source],
                device_id={"snap": source},
                device_id_type=MESH,
            ).wait_recv()
        for c in (0, 1):
            size = SNAPS * BATCHES[b]
            own = pl.ds(me * BLOCKS + firsts[b] // EDGE, size // EDGE)
            bufs[c][own] = zin[c, firsts[b] : firsts[b] + size].reshape(size // EDGE, EDGE, LANES)

    def cell(gates, state_c):
        i, f, g, o = (gates[:, q * HIDDEN : (q + 1) * HIDDEN] for q in range(4))
        state_c = sigmoid(f) * state_c + sigmoid(i) * jnp.tanh(g)
        return sigmoid(o) * jnp.tanh(state_c), state_c

    def begin(b):
        return cell(pre[b][: BATCHES[b]], jnp.zeros((BATCHES[b], HIDDEN), F32))

    def product(h):
        high, low = halves(h)
        both = dot(jnp.concatenate([high, low], axis=0), rec_high[...])
        rows = h.shape[0]
        return both[:rows] + (both[rows:] + dot(high, rec_low[...]))

    def steps(b, start, stop, carry):
        def advance(s, carry):
            h, state_c = carry
            wide = product(h)
            rows = pl.ds(pl.multiple_of(s * BATCHES[b], 16), BATCHES[b])
            new = cell(pre[b][rows] + wide[:, : 4 * HIDDEN], state_c)
            z_start(b, s - 1, wide[:, 4 * HIDDEN :])
            return new

        return lax.fori_loop(start, stop, advance, carry)

    def finish(b, carry):
        last = slice(4 * HIDDEN, 5 * HIDDEN)
        z_start(b, SNAPS - 1, dot3(carry[0], rec_high[:, last], rec_low[:, last]))

    split_tiles(0, 4)
    one[0].ring()
    split_tiles(4, 8)
    for copy in weights:
        copy.wait()
    in_high[...], in_low[...] = halves(w_in[...])
    rec_high[:, : 4 * HIDDEN], rec_low[:, : 4 * HIDDEN] = halves(w_rec[...])
    rec_high[:, 4 * HIDDEN :], rec_low[:, 4 * HIDDEN :] = halves(w_two[...])
    one[0].onward(0)
    one[0].opposite()
    one[1].own()
    one[0].onward(-1)
    one[0].onward(1)
    one[1].ring()
    one[0].onward(2)
    one[1].onward(0)
    one[1].opposite()
    one[0].last()

    conv(0, 0, EARLY, True)
    x_start(0, 0)
    one[1].onward(-1)
    one[1].onward(1)
    conv(0, EARLY, BLOCKS, True)
    x_start(0, 1)
    one[1].onward(2)
    x_wait(0, 0)
    x_wait(0, 1)
    one[1].last()

    conv(1, 0, EARLY, True)
    x_start(1, 0)
    conv(1, EARLY, BLOCKS, True)
    x_start(1, 1)

    x_wait(1, 0)
    input_product(0)
    finish(0, steps(0, 1, SNAPS, begin(0)))
    one[0].wait_sent()
    one[1].wait_sent()
    for device in beside:
        pl.semaphore_signal(free_sem, inc=1, device_id={"vtx": device}, device_id_type=MESH)
    x_wait(1, 1)
    input_product(1)
    z_wait(0)
    pl.semaphore_wait(free_sem, len(beside))
    two = [
        [
            Gather(bufs[c], first, count, g_send, g_recv, (2 + 2 * b + c) * GATHER_SEMS)
            for c in (0, 1)
        ]
        for b, (first, count) in enumerate(((0, EARLY), (EARLY, BLOCKS - EARLY)))
    ]
    two[0][0].own()
    two[0][1].own()
    carry = steps(1, 1, 8, begin(1))
    two[0][0].ring()
    two[0][1].ring()
    finish(1, steps(1, 8, SNAPS, carry))
    two[0][0].onward(0)
    two[0][0].opposite()
    two[0][1].onward(0)
    two[0][1].opposite()
    for da in (-1, 1, 2):
        two[0][0].onward(da)
        two[0][1].onward(da)
    z_wait(1)
    two[1][0].own()
    two[1][1].own()
    two[0][0].last()
    two[0][1].last()
    two[1][0].ring()
    two[1][0].onward(0)
    two[1][0].opposite()
    two[1][1].ring()
    two[1][0].onward(-1)
    two[1][0].onward(1)
    two[1][1].onward(0)
    two[1][1].opposite()
    two[1][0].onward(2)
    two[1][0].last()
    conv(0, 0, 4, False)
    two[1][1].onward(-1)
    two[1][1].onward(1)
    conv(0, 4, 8, False)
    two[1][1].onward(2)
    two[1][1].last()
    conv(1, 0, 8, False)

    for b in (0, 1):
        for c in (0, 1):
            two[b][c].wait_sent()
    for copy in x_sent:
        copy.wait_send()
    for b in (0, 1):
        for device in others:
            z_copy(b, device).wait_send()


def on_device(feats, col_ids, tiles, w_first, w_input, w_recur, lstm_bias, w_second):
    everyone = (lax.axis_size("vtx") * BLOCKS, EDGE, LANES)
    vmem, hbm = pl.BlockSpec(memory_space=pltpu.VMEM), pl.BlockSpec(memory_space=pl.ANY)
    dma = pltpu.SemaphoreType.DMA
    out = pl.pallas_call(
        kernel,
        in_specs=[pl.BlockSpec(memory_space=pltpu.SMEM), vmem, *[hbm] * 6],
        out_specs=vmem,
        out_shape=pltpu.VMEM((ROWS, HIDDEN), F32),
        scratch_shapes=[
            pltpu.VMEM(everyone, F32),
            pltpu.VMEM(everyone, F32),
            pltpu.VMEM((BLOCKS, KT, EDGE, EDGE), F32),
            pltpu.VMEM((BLOCKS, 2 * EDGE, KT * EDGE), BF16),
            pltpu.VMEM((BLOCKS, EDGE, LANES), F32),
            pltpu.VMEM((KT * EDGE, 2 * LANES), BF16),
            pltpu.VMEM((2, ROWS, LANES), F32),
            *[pltpu.VMEM((2, SNAPS, batch, LANES), F32) for batch in BATCHES],
            *[pltpu.VMEM((SNAPS * batch, 4 * HIDDEN), F32) for batch in BATCHES],
            *[pltpu.VMEM((SNAPS, 2, batch, LANES), F32) for batch in BATCHES],
            pltpu.VMEM((2, ROWS, LANES), F32),
            pltpu.VMEM(feats.shape[1:], F32),
            pltpu.VMEM(w_first.shape, F32),
            pltpu.VMEM((HIDDEN, 4 * HIDDEN), F32),
            pltpu.VMEM((HIDDEN, 4 * HIDDEN), F32),
            pltpu.VMEM((HIDDEN, HIDDEN), F32),
            pltpu.VMEM((HIDDEN, 4 * HIDDEN), BF16),
            pltpu.VMEM((HIDDEN, 4 * HIDDEN), BF16),
            pltpu.VMEM((HIDDEN, 5 * HIDDEN), BF16),
            pltpu.VMEM((HIDDEN, 5 * HIDDEN), BF16),
            dma((6 * GATHER_SEMS,)),
            dma((6 * GATHER_SEMS,)),
            dma((2, 2, SNAPS)),
            dma((2, 2, SNAPS)),
            dma((2, SNAPS)),
            dma((2, SNAPS)),
            dma((2,)),
            dma((BLOCKS,)),
            dma((BLOCKS + 2,)),
            dma((3,)),
            pltpu.SemaphoreType.REGULAR,
        ],
        compiler_params=pltpu.CompilerParams(
            collective_id=0, has_side_effects=True, vmem_limit_bytes=56 << 20
        ),
    )(
        col_ids[0], lstm_bias.reshape(1, -1), feats[0], w_first, tiles[0], w_input, w_recur, w_second
    )
    return out[None]


def solution(mesh):
    placed = (
        P("snap", "vtx", None),
        P("snap", "vtx", None),
        P("snap", "vtx", None, None, None),
        P(),
        P(),
        P(),
        P(),
        P(),
    )
    return jax.shard_map(
        on_device, mesh=mesh, in_specs=placed, out_specs=P("snap", "vtx", None), check_vma=False
    )
```

```python
import jax
import jax.numpy as jnp
from jax import lax
from jax.experimental import pallas as pl
from jax.experimental.pallas import tpu as pltpu
from jax.sharding import PartitionSpec as P

BF16, F32 = jnp.bfloat16, jnp.float32
MESH = pl.DeviceIdType.MESH
SIDE = 4
SNAPS = 16
EDGE = 128
LANES = 128
KT = 16
BLOCKS = 8
BATCHES = (16, 48)
ROWS = 1024
EARLY = SNAPS * BATCHES[0] // EDGE
HIDDEN = 256
GATHER_SEMS = 40


def halves(x):
    high = x.astype(BF16)
    return high, (x - high.astype(F32)).astype(BF16)


def dot(a, b):
    return jnp.dot(a, b, preferred_element_type=F32)


def dot3(a, b_high, b_low):
    a_high, a_low = halves(a)
    return dot(a_high, b_high) + (dot(a_low, b_high) + dot(a_high, b_low))


def sigmoid(x):
    return 0.5 * jnp.tanh(0.5 * x) + 0.5


class Gather:
    def __init__(self, buffer, first, count, send_sem, recv_sem, base):
        self.buffer, self.first, self.count = buffer, first, count
        self.send_sem, self.recv_sem, self.base = send_sem, recv_sem, base
        me = lax.axis_index("vtx")
        self.x, self.y = lax.rem(me, SIDE), lax.div(me, SIDE)
        self.me = me
        self.started = []

    def device(self, half, da, db):
        dx, dy = (da, db) if half == 0 else (db, da)
        return lax.rem(self.y + (dy + SIDE), SIDE) * SIDE + lax.rem(self.x + (dx + SIDE), SIDE)

    def place(self, half, da, db, part):
        size = self.count // 2
        block = self.device(half, da, db) * BLOCKS + (self.first + half * size)
        if part is None:
            return self.buffer.at[pl.ds(block, size)]
        return self.buffer.at[pl.ds(block, size), pl.ds(part * (EDGE // 2), EDGE // 2)]

    def number(self, half, da, db, part):
        along = {-1: 0, 1: 1, 2: 2}
        if db == 0:
            number = along[da]
            number += part or 0
        else:
            number = 4 + 4 * (0, -1, 1, 2).index(da) + along[db] + (part or 0)
        return self.base + half * 20 + number

    def copy(self, half, axis, way, da, db, part):
        seen = lambda d: 2 if d in (-1, 1) and d == -way else -way
        if axis == 0:
            to, number = self.device(half, way, 0), self.number(half, seen(da), db, part)
        else:
            to, number = self.device(half, 0, way), self.number(half, da, seen(db), part)
        place = self.place(half, da, db, part)
        return pltpu.make_async_remote_copy(
            src_ref=place,
            dst_ref=place,
            send_sem=self.send_sem.at[number],
            recv_sem=self.recv_sem.at[number],
            device_id={"vtx": to},
            device_id_type=MESH,
        )

    def send(self, half, axis, way, da, db, part=None):
        copy = self.copy(half, axis, way, da, db, part)
        copy.start()
        self.started.append(copy)

    def wait(self, half, da, db, part=None):
        number = self.number(half, da, db, part)
        place = self.place(half, da, db, part)
        pltpu.make_async_remote_copy(
            src_ref=place,
            dst_ref=place,
            send_sem=self.send_sem.at[number],
            recv_sem=self.recv_sem.at[number],
            device_id={"vtx": self.device(half, 1, 0)},
            device_id_type=MESH,
        ).wait_recv()

    def both(self, half, da):
        for way in (1, -1):
            self.send(half, 1, way, da, 0)

    def own_half(self, half):
        for way in (1, -1):
            self.send(half, 0, way, 0, 0)
        self.both(half, 0)

    def own(self):
        for half in (0, 1):
            for way in (1, -1):
                self.send(half, 0, way, 0, 0)
        for half in (0, 1):
            self.both(half, 0)

    def ring(self):
        for half in (0, 1):
            self.wait(half, -1, 0)
            self.send(half, 0, 1, -1, 0, 0)
            self.wait(half, 1, 0)
            self.send(half, 0, -1, 1, 0, 1)
        for half in (0, 1):
            self.both(half, -1)
            self.both(half, 1)

    def onward(self, da):
        for half in (0, 1):
            self.wait(half, da, -1)
            self.send(half, 1, 1, da, -1, 0)
            self.wait(half, da, 1)
            self.send(half, 1, -1, da, 1, 1)

    def opposite(self):
        for half in (0, 1):
            self.wait(half, 2, 0, 0)
            self.wait(half, 2, 0, 1)
            self.both(half, 2)

    def last(self):
        for da in (0, -1, 1, 2):
            for half in (0, 1):
                for part in (0, 1):
                    self.wait(half, da, 2, part)

    def wait_sent(self):
        for copy in self.started:
            copy.wait_send()


def kernel(
    ids_ref, bias_ref, feats_hbm, w_first_hbm, tiles_hbm, w_in_hbm, w_rec_hbm, w_two_hbm, out_ref,
    buf0, buf1, staged, tcat, scales, ycat, hid, xin0, xin1, pre0, pre1, zout0, zout1, zin,
    feats, w_first, w_in, w_rec, w_two, in_high, in_low, rec_high, rec_low,
    g_send, g_recv, x_send, x_recv, z_send, z_recv, local_sem, tile_sem, feats_sem, weight_sem, free_sem,
):
    snap, me = lax.axis_index("snap"), lax.axis_index("vtx")
    x, y = lax.rem(me, SIDE), lax.div(me, SIDE)
    bufs, xin, pre, zout = (buf0, buf1), (xin0, xin1), (pre0, pre1), (zout0, zout1)
    firsts = (0, SNAPS * BATCHES[0])
    others = [lax.rem(snap + k, SNAPS) for k in range(1, SNAPS)]
    beside = [
        lax.rem(y + dy, SIDE) * SIDE + lax.rem(x + dx, SIDE)
        for dx, dy in ((1, 0), (SIDE - 1, 0), (0, 1), (0, SIDE - 1))
    ]

    weights = [
        pltpu.make_async_copy(a, b, weight_sem.at[i])
        for i, (a, b) in enumerate(((w_in_hbm, w_in), (w_rec_hbm, w_rec), (w_two_hbm, w_two)))
    ]
    first_copies = [
        pltpu.make_async_copy(w_first_hbm.at[rows], w_first.at[rows], feats_sem.at[BLOCKS + i])
        for i, rows in enumerate((slice(0, HIDDEN), slice(HIDDEN, 2 * HIDDEN)))
    ]
    feats_copies = [
        pltpu.make_async_copy(feats_hbm.at[rows], feats.at[rows], feats_sem.at[r])
        for r, rows in enumerate(slice(r * EDGE, (r + 1) * EDGE) for r in range(BLOCKS))
    ]

    def tile_copy(r):
        return pltpu.make_async_copy(tiles_hbm.at[r], staged.at[r], tile_sem.at[r])

    for copy in (*first_copies, *feats_copies):
        copy.start()
    barrier = pltpu.get_barrier_semaphore()
    for device in beside:
        pl.semaphore_signal(barrier, inc=1, device_id={"vtx": device}, device_id_type=MESH)
    for device in others:
        pl.semaphore_signal(barrier, inc=1, device_id={"snap": device}, device_id_type=MESH)

    one = [Gather(bufs[c], 0, BLOCKS, g_send, g_recv, c * GATHER_SEMS) for c in (0, 1)]
    for copy in first_copies:
        copy.wait()

    def first_product(c, half):
        high, low = halves(w_first[:, c * LANES : (c + 1) * LANES])
        for r in range(4 * half, 4 * half + 4):
            if c == 0:
                feats_copies[r].wait()
            bufs[c][me * BLOCKS + r] = dot3(feats[r * EDGE : (r + 1) * EDGE, :], high, low)

    first_product(0, 0)
    pl.semaphore_wait(barrier, len(beside) + len(others))
    one[0].own_half(0)
    first_product(0, 1)
    one[0].own_half(1)
    for r in range(BLOCKS):
        tile_copy(r).start()
    for copy in weights:
        copy.start()
    first_product(1, 0)
    first_product(1, 1)

    def split_tiles(start, stop):
        def block(r, _):
            tile_copy(r).wait()
            squares = jnp.zeros((EDGE, EDGE), F32)
            for k in range(KT):
                tile = staged[r, k]
                squares += tile * tile
                high, low = halves(tile)
                tcat[r, :EDGE, k * EDGE : (k + 1) * EDGE] = high
                tcat[r, EDGE:, k * EDGE : (k + 1) * EDGE] = low
            scale = lax.rsqrt(1.0 + jnp.sum(squares, axis=1, keepdims=True))
            scales[r] = jnp.broadcast_to(scale, (EDGE, LANES))
            return 0

        lax.fori_loop(start, stop, block, 0)

    def conv(c, start, stop, first):
        def block(r, _):
            for k in range(KT):
                high, low = halves(bufs[c][ids_ref[r, k]])
                ycat[k * EDGE : (k + 1) * EDGE, :LANES] = high
                ycat[k * EDGE : (k + 1) * EDGE, LANES:] = low
            out = dot(tcat[r], ycat[...])
            total = (out[:EDGE, :LANES] + out[:EDGE, LANES:]) + (out[EDGE:, :LANES] + out[EDGE:, LANES:])
            rows = pl.ds(pl.multiple_of(r * EDGE, EDGE), EDGE)
            total = scales[r] * (bufs[c][me * BLOCKS + r] + total)
            if first:
                hid[c, rows] = jnp.maximum(total, 0.0)
            else:
                out_ref[rows, c * LANES : (c + 1) * LANES] = total
            return 0

        lax.fori_loop(start, stop, block, 0)

    def shares(ref, c, b, j):
        return ref.at[c, pl.ds(pl.multiple_of(firsts[b] + j * BATCHES[b], 16), BATCHES[b])]

    x_sent = []

    def x_copy(c, b, k):
        to = others[k - 1]
        return pltpu.make_async_remote_copy(
            src_ref=shares(hid, c, b, to),
            dst_ref=xin[b].at[c, snap],
            send_sem=x_send.at[c, b, k],
            recv_sem=x_recv.at[c, b, k],
            device_id={"snap": to},
            device_id_type=MESH,
        )

    def x_local(c, b):
        return pltpu.make_async_copy(shares(hid, c, b, snap), xin[b].at[c, snap], x_send.at[c, b, 0])

    def x_start(c, b):
        for k in range(1, SNAPS):
            copy = x_copy(c, b, k)
            copy.start()
            x_sent.append(copy)
        x_local(c, b).start()

    def x_wait(c, b):
        x_local(c, b).wait()
        for k in range(1, SNAPS):
            source = lax.rem(snap + (SNAPS - k), SNAPS)
            pltpu.make_async_remote_copy(
                src_ref=xin[b].at[c, source],
                dst_ref=xin[b].at[c, source],
                send_sem=x_send.at[c, b, k],
                recv_sem=x_recv.at[c, b, k],
                device_id={"snap": source},
                device_id_type=MESH,
            ).wait_recv()

    def input_product(b):
        count = 256 // BATCHES[b] if b == 0 else 4
        size = count * BATCHES[b]

        def some(i, _):
            rows = pl.ds(pl.multiple_of(i * size, size), size)
            steps = pl.ds(i * count, count)
            both = [xin[b][c, steps].reshape(size, LANES) for c in (0, 1)]
            pre[b][rows] = dot3(jnp.concatenate(both, axis=1), in_high[...], in_low[...]) + bias_ref[...]
            return 0

        lax.fori_loop(0, SNAPS // count, some, 0)

    def z_copy(b, s):
        return pltpu.make_async_remote_copy(
            src_ref=zout[b].at[s],
            dst_ref=shares(zin, slice(None), b, snap),
            send_sem=z_send.at[b, s],
            recv_sem=z_recv.at[b, snap],
            device_id={"snap": s},
            device_id_type=MESH,
        )

    def z_local(b):
        return pltpu.make_async_copy(zout[b].at[snap], shares(zin, slice(None), b, snap), local_sem.at[b])

    def z_start(b, s, z):
        zout[b][s, 0] = z[:, :LANES]
        zout[b][s, 1] = z[:, LANES:]

        @pl.when(s != snap)
        def _():
            z_copy(b, s).start()

        @pl.when(s == snap)
        def _():
            z_local(b).start()

    def z_wait(b):
        z_local(b).wait()
        for source in others:
            pltpu.make_async_remote_copy(
                src_ref=shares(zin, slice(None), b, source),
                dst_ref=shares(zin, slice(None), b, source),
                send_sem=z_send.at[b, source],
                recv_sem=z_recv.at[b, source],
                device_id={"snap": source},
                device_id_type=MESH,
            ).wait_recv()
        for c in (0, 1):
            size = SNAPS * BATCHES[b]
            own = pl.ds(me * BLOCKS + firsts[b] // EDGE, size // EDGE)
            bufs[c][own] = zin[c, firsts[b] : firsts[b] + size].reshape(size // EDGE, EDGE, LANES)

    def cell(gates, state_c):
        i, f, g, o = (gates[:, q * HIDDEN : (q + 1) * HIDDEN] for q in range(4))
        state_c = sigmoid(f) * state_c + sigmoid(i) * jnp.tanh(g)
        return sigmoid(o) * jnp.tanh(state_c), state_c

    def begin(b):
        return cell(pre[b][: BATCHES[b]], jnp.zeros((BATCHES[b], HIDDEN), F32))

    def product(h):
        high, low = halves(h)
        both = dot(jnp.concatenate([high, low], axis=0), rec_high[...])
        rows = h.shape[0]
        return both[:rows] + (both[rows:] + dot(high, rec_low[...]))

    def steps(b, start, stop, carry):
        def advance(s, carry):
            h, state_c = carry
            wide = product(h)
            rows = pl.ds(pl.multiple_of(s * BATCHES[b], 16), BATCHES[b])
            new = cell(pre[b][rows] + wide[:, : 4 * HIDDEN], state_c)
            z_start(b, s - 1, wide[:, 4 * HIDDEN :])
            return new

        return lax.fori_loop(start, stop, advance, carry)

    def finish(b, carry):
        last = slice(4 * HIDDEN, 5 * HIDDEN)
        z_start(b, SNAPS - 1, dot3(carry[0], rec_high[:, last], rec_low[:, last]))

    split_tiles(0, 4)
    one[0].ring()
    split_tiles(4, 8)
    for copy in weights:
        copy.wait()
    in_high[...], in_low[...] = halves(w_in[...])
    rec_high[:, : 4 * HIDDEN], rec_low[:, : 4 * HIDDEN] = halves(w_rec[...])
    rec_high[:, 4 * HIDDEN :], rec_low[:, 4 * HIDDEN :] = halves(w_two[...])
    one[0].onward(0)
    one[0].opposite()
    one[1].own()
    one[0].onward(-1)
    one[0].onward(1)
    one[1].ring()
    one[0].onward(2)
    one[1].onward(0)
    one[1].opposite()
    one[0].last()

    conv(0, 0, EARLY, True)
    x_start(0, 0)
    conv(0, EARLY, 4, True)
    one[1].onward(-1)
    one[1].onward(1)
    conv(0, 4, BLOCKS, True)
    x_start(0, 1)
    one[1].onward(2)
    x_wait(0, 0)
    x_wait(0, 1)
    one[1].last()

    conv(1, 0, EARLY, True)
    x_start(1, 0)
    conv(1, EARLY, BLOCKS, True)
    x_start(1, 1)

    x_wait(1, 0)
    input_product(0)
    finish(0, steps(0, 1, SNAPS, begin(0)))
    one[0].wait_sent()
    one[1].wait_sent()
    for device in beside:
        pl.semaphore_signal(free_sem, inc=1, device_id={"vtx": device}, device_id_type=MESH)
    x_wait(1, 1)
    input_product(1)
    z_wait(0)
    pl.semaphore_wait(free_sem, len(beside))
    two = [
        [
            Gather(bufs[c], first, count, g_send, g_recv, (2 + 2 * b + c) * GATHER_SEMS)
            for c in (0, 1)
        ]
        for b, (first, count) in enumerate(((0, EARLY), (EARLY, BLOCKS - EARLY)))
    ]
    two[0][0].own()
    two[0][1].own()
    finish(1, steps(1, 1, SNAPS, begin(1)))
    two[0][0].ring()
    two[0][1].ring()
    two[0][0].onward(0)
    two[0][0].opposite()
    two[0][1].onward(0)
    two[0][1].opposite()
    for da in (-1, 1, 2):
        two[0][0].onward(da)
        two[0][1].onward(da)
    z_wait(1)
    two[1][0].own()
    two[1][1].own()
    two[0][0].last()
    two[0][1].last()
    two[1][0].ring()
    two[1][0].onward(0)
    two[1][0].opposite()
    two[1][1].ring()
    two[1][0].onward(-1)
    two[1][0].onward(1)
    two[1][1].onward(0)
    two[1][1].opposite()
    two[1][0].onward(2)
    two[1][0].last()
    conv(0, 0, 4, False)
    two[1][1].onward(-1)
    two[1][1].onward(1)
    conv(0, 4, 8, False)
    two[1][1].onward(2)
    two[1][1].last()
    conv(1, 0, 8, False)

    for b in (0, 1):
        for c in (0, 1):
            two[b][c].wait_sent()
    for copy in x_sent:
        copy.wait_send()
    for b in (0, 1):
        for device in others:
            z_copy(b, device).wait_send()


def on_device(feats, col_ids, tiles, w_first, w_input, w_recur, lstm_bias, w_second):
    everyone = (lax.axis_size("vtx") * BLOCKS, EDGE, LANES)
    vmem, hbm = pl.BlockSpec(memory_space=pltpu.VMEM), pl.BlockSpec(memory_space=pl.ANY)
    dma = pltpu.SemaphoreType.DMA
    out = pl.pallas_call(
        kernel,
        in_specs=[pl.BlockSpec(memory_space=pltpu.SMEM), vmem, *[hbm] * 6],
        out_specs=vmem,
        out_shape=pltpu.VMEM((ROWS, HIDDEN), F32),
        scratch_shapes=[
            pltpu.VMEM(everyone, F32),
            pltpu.VMEM(everyone, F32),
            pltpu.VMEM((BLOCKS, KT, EDGE, EDGE), F32),
            pltpu.VMEM((BLOCKS, 2 * EDGE, KT * EDGE), BF16),
            pltpu.VMEM((BLOCKS, EDGE, LANES), F32),
            pltpu.VMEM((KT * EDGE, 2 * LANES), BF16),
            pltpu.VMEM((2, ROWS, LANES), F32),
            *[pltpu.VMEM((2, SNAPS, batch, LANES), F32) for batch in BATCHES],
            *[pltpu.VMEM((SNAPS * batch, 4 * HIDDEN), F32) for batch in BATCHES],
            *[pltpu.VMEM((SNAPS, 2, batch, LANES), F32) for batch in BATCHES],
            pltpu.VMEM((2, ROWS, LANES), F32),
            pltpu.VMEM(feats.shape[1:], F32),
            pltpu.VMEM(w_first.shape, F32),
            pltpu.VMEM((HIDDEN, 4 * HIDDEN), F32),
            pltpu.VMEM((HIDDEN, 4 * HIDDEN), F32),
            pltpu.VMEM((HIDDEN, HIDDEN), F32),
            pltpu.VMEM((HIDDEN, 4 * HIDDEN), BF16),
            pltpu.VMEM((HIDDEN, 4 * HIDDEN), BF16),
            pltpu.VMEM((HIDDEN, 5 * HIDDEN), BF16),
            pltpu.VMEM((HIDDEN, 5 * HIDDEN), BF16),
            dma((6 * GATHER_SEMS,)),
            dma((6 * GATHER_SEMS,)),
            dma((2, 2, SNAPS)),
            dma((2, 2, SNAPS)),
            dma((2, SNAPS)),
            dma((2, SNAPS)),
            dma((2,)),
            dma((BLOCKS,)),
            dma((BLOCKS + 2,)),
            dma((3,)),
            pltpu.SemaphoreType.REGULAR,
        ],
        compiler_params=pltpu.CompilerParams(
            collective_id=0, has_side_effects=True, vmem_limit_bytes=56 << 20
        ),
    )(
        col_ids[0], lstm_bias.reshape(1, -1), feats[0], w_first, tiles[0], w_input, w_recur, w_second
    )
    return out[None]


def solution(mesh):
    placed = (
        P("snap", "vtx", None),
        P("snap", "vtx", None),
        P("snap", "vtx", None, None, None),
        P(),
        P(),
        P(),
        P(),
        P(),
    )
    return jax.shard_map(
        on_device, mesh=mesh, in_specs=placed, out_specs=P("snap", "vtx", None), check_vma=False
    )
```

```python
import jax
import jax.numpy as jnp
from jax import lax
from jax.experimental import pallas as pl
from jax.experimental.pallas import tpu as pltpu
from jax.sharding import PartitionSpec as P

BF16, F32 = jnp.bfloat16, jnp.float32
MESH = pl.DeviceIdType.MESH
SIDE = 4
SNAPS = 16
EDGE = 128
LANES = 128
KT = 16
BLOCKS = 8
BATCHES = (16, 48)
ROWS = 1024
EARLY = SNAPS * BATCHES[0] // EDGE
HIDDEN = 256
GATHER_SEMS = 40


def halves(x):
    high = x.astype(BF16)
    return high, (x - high.astype(F32)).astype(BF16)


def dot(a, b):
    return jnp.dot(a, b, preferred_element_type=F32)


def dot3(a, b_high, b_low):
    a_high, a_low = halves(a)
    return dot(a_high, b_high) + (dot(a_low, b_high) + dot(a_high, b_low))


def sigmoid(x):
    return 0.5 * jnp.tanh(0.5 * x) + 0.5


class Gather:
    def __init__(self, buffer, first, count, send_sem, recv_sem, base):
        self.buffer, self.first, self.count = buffer, first, count
        self.send_sem, self.recv_sem, self.base = send_sem, recv_sem, base
        me = lax.axis_index("vtx")
        self.x, self.y = lax.rem(me, SIDE), lax.div(me, SIDE)
        self.me = me
        self.started = []

    def device(self, half, da, db):
        dx, dy = (da, db) if half == 0 else (db, da)
        return lax.rem(self.y + (dy + SIDE), SIDE) * SIDE + lax.rem(self.x + (dx + SIDE), SIDE)

    def place(self, half, da, db, part):
        size = self.count // 2
        block = self.device(half, da, db) * BLOCKS + (self.first + half * size)
        if part is None:
            return self.buffer.at[pl.ds(block, size)]
        return self.buffer.at[pl.ds(block, size), pl.ds(part * (EDGE // 2), EDGE // 2)]

    def number(self, half, da, db, part):
        along = {-1: 0, 1: 1, 2: 2}
        if db == 0:
            number = along[da]
            number += part or 0
        else:
            number = 4 + 4 * (0, -1, 1, 2).index(da) + along[db] + (part or 0)
        return self.base + half * 20 + number

    def copy(self, half, axis, way, da, db, part):
        seen = lambda d: 2 if d in (-1, 1) and d == -way else -way
        if axis == 0:
            to, number = self.device(half, way, 0), self.number(half, seen(da), db, part)
        else:
            to, number = self.device(half, 0, way), self.number(half, da, seen(db), part)
        place = self.place(half, da, db, part)
        return pltpu.make_async_remote_copy(
            src_ref=place,
            dst_ref=place,
            send_sem=self.send_sem.at[number],
            recv_sem=self.recv_sem.at[number],
            device_id={"vtx": to},
            device_id_type=MESH,
        )

    def send(self, half, axis, way, da, db, part=None):
        copy = self.copy(half, axis, way, da, db, part)
        copy.start()
        self.started.append(copy)

    def wait(self, half, da, db, part=None):
        number = self.number(half, da, db, part)
        place = self.place(half, da, db, part)
        pltpu.make_async_remote_copy(
            src_ref=place,
            dst_ref=place,
            send_sem=self.send_sem.at[number],
            recv_sem=self.recv_sem.at[number],
            device_id={"vtx": self.device(half, 1, 0)},
            device_id_type=MESH,
        ).wait_recv()

    def both(self, half, da):
        for way in (1, -1):
            self.send(half, 1, way, da, 0)

    def own_half(self, half):
        for way in (1, -1):
            self.send(half, 0, way, 0, 0)
        self.both(half, 0)

    def own(self):
        for half in (0, 1):
            for way in (1, -1):
                self.send(half, 0, way, 0, 0)
        for half in (0, 1):
            self.both(half, 0)

    def ring(self):
        for half in (0, 1):
            self.wait(half, -1, 0)
            self.send(half, 0, 1, -1, 0, 0)
            self.wait(half, 1, 0)
            self.send(half, 0, -1, 1, 0, 1)
        for half in (0, 1):
            self.both(half, -1)
            self.both(half, 1)

    def onward(self, da):
        for half in (0, 1):
            self.wait(half, da, -1)
            self.send(half, 1, 1, da, -1, 0)
            self.wait(half, da, 1)
            self.send(half, 1, -1, da, 1, 1)

    def opposite(self):
        for half in (0, 1):
            self.wait(half, 2, 0, 0)
            self.wait(half, 2, 0, 1)
            self.both(half, 2)

    def last(self):
        for da in (0, -1, 1, 2):
            for half in (0, 1):
                for part in (0, 1):
                    self.wait(half, da, 2, part)

    def wait_sent(self):
        for copy in self.started:
            copy.wait_send()


def kernel(
    ids_ref, bias_ref, feats_hbm, w_first_hbm, tiles_hbm, w_in_hbm, w_rec_hbm, w_two_hbm, out_ref,
    buf0, buf1, staged, tcat, scales, ycat, hid, xin0, xin1, pre0, pre1, zout0, zout1, zin,
    feats, w_first, w_in, w_rec, w_two, in_high, in_low, rec_high, rec_low,
    g_send, g_recv, x_send, x_recv, z_send, z_recv, local_sem, tile_sem, feats_sem, weight_sem, free_sem,
):
    snap, me = lax.axis_index("snap"), lax.axis_index("vtx")
    x, y = lax.rem(me, SIDE), lax.div(me, SIDE)
    bufs, xin, pre, zout = (buf0, buf1), (xin0, xin1), (pre0, pre1), (zout0, zout1)
    firsts = (0, SNAPS * BATCHES[0])
    others = [lax.rem(snap + k, SNAPS) for k in range(1, SNAPS)]
    beside = [
        lax.rem(y + dy, SIDE) * SIDE + lax.rem(x + dx, SIDE)
        for dx, dy in ((1, 0), (SIDE - 1, 0), (0, 1), (0, SIDE - 1))
    ]

    weights = [
        pltpu.make_async_copy(a, b, weight_sem.at[i])
        for i, (a, b) in enumerate(((w_in_hbm, w_in), (w_rec_hbm, w_rec), (w_two_hbm, w_two)))
    ]
    first_copies = [
        pltpu.make_async_copy(w_first_hbm.at[rows], w_first.at[rows], feats_sem.at[BLOCKS + i])
        for i, rows in enumerate((slice(0, HIDDEN), slice(HIDDEN, 2 * HIDDEN)))
    ]
    feats_copies = [
        pltpu.make_async_copy(feats_hbm.at[rows], feats.at[rows], feats_sem.at[r])
        for r, rows in enumerate(slice(r * EDGE, (r + 1) * EDGE) for r in range(BLOCKS))
    ]

    def tile_copy(r):
        return pltpu.make_async_copy(tiles_hbm.at[r], staged.at[r], tile_sem.at[r])

    for copy in (*first_copies, *feats_copies):
        copy.start()
    barrier = pltpu.get_barrier_semaphore()
    for device in beside:
        pl.semaphore_signal(barrier, inc=1, device_id={"vtx": device}, device_id_type=MESH)
    for device in others:
        pl.semaphore_signal(barrier, inc=1, device_id={"snap": device}, device_id_type=MESH)

    one = [Gather(bufs[c], 0, BLOCKS, g_send, g_recv, c * GATHER_SEMS) for c in (0, 1)]
    for copy in first_copies:
        copy.wait()

    def first_product(c, half):
        high, low = halves(w_first[:, c * LANES : (c + 1) * LANES])
        for r in range(4 * half, 4 * half + 4):
            if c == 0:
                feats_copies[r].wait()
            bufs[c][me * BLOCKS + r] = dot3(feats[r * EDGE : (r + 1) * EDGE, :], high, low)

    first_product(0, 0)
    pl.semaphore_wait(barrier, len(beside) + len(others))
    one[0].own_half(0)
    first_product(0, 1)
    one[0].own_half(1)
    for r in range(BLOCKS):
        tile_copy(r).start()
    for copy in weights:
        copy.start()
    first_product(1, 0)
    first_product(1, 1)

    def split_tiles(start, stop):
        def block(r, _):
            tile_copy(r).wait()
            squares = jnp.zeros((EDGE, EDGE), F32)
            for k in range(KT):
                tile = staged[r, k]
                squares += tile * tile
                high, low = halves(tile)
                tcat[r, :EDGE, k * EDGE : (k + 1) * EDGE] = high
                tcat[r, EDGE:, k * EDGE : (k + 1) * EDGE] = low
            scale = lax.rsqrt(1.0 + jnp.sum(squares, axis=1, keepdims=True))
            scales[r] = jnp.broadcast_to(scale, (EDGE, LANES))
            return 0

        lax.fori_loop(start, stop, block, 0)

    def conv(c, start, stop, first):
        def one_block(r, slot):
            for k in range(KT):
                high, low = halves(bufs[c][ids_ref[r, k]])
                ycat[slot, k * EDGE : (k + 1) * EDGE, :LANES] = high
                ycat[slot, k * EDGE : (k + 1) * EDGE, LANES:] = low
            out = dot(tcat[r], ycat[slot])
            total = (out[:EDGE, :LANES] + out[:EDGE, LANES:]) + (out[EDGE:, :LANES] + out[EDGE:, LANES:])
            rows = pl.ds(pl.multiple_of(r * EDGE, EDGE), EDGE)
            total = scales[r] * (bufs[c][me * BLOCKS + r] + total)
            if first:
                hid[c, rows] = jnp.maximum(total, 0.0)
            else:
                out_ref[rows, c * LANES : (c + 1) * LANES] = total

        def pair(i, _):
            for slot in (0, 1):
                one_block(start + 2 * i + slot, slot)
            return 0

        lax.fori_loop(0, (stop - start) // 2, pair, 0)

    def shares(ref, c, b, j):
        return ref.at[c, pl.ds(pl.multiple_of(firsts[b] + j * BATCHES[b], 16), BATCHES[b])]

    x_sent = []

    def x_copy(c, b, k):
        to = others[k - 1]
        return pltpu.make_async_remote_copy(
            src_ref=shares(hid, c, b, to),
            dst_ref=xin[b].at[c, snap],
            send_sem=x_send.at[c, b, k],
            recv_sem=x_recv.at[c, b, k],
            device_id={"snap": to},
            device_id_type=MESH,
        )

    def x_local(c, b):
        return pltpu.make_async_copy(shares(hid, c, b, snap), xin[b].at[c, snap], x_send.at[c, b, 0])

    def x_start(c, b):
        for k in range(1, SNAPS):
            copy = x_copy(c, b, k)
            copy.start()
            x_sent.append(copy)
        x_local(c, b).start()

    def x_wait(c, b):
        x_local(c, b).wait()
        for k in range(1, SNAPS):
            source = lax.rem(snap + (SNAPS - k), SNAPS)
            pltpu.make_async_remote_copy(
                src_ref=xin[b].at[c, source],
                dst_ref=xin[b].at[c, source],
                send_sem=x_send.at[c, b, k],
                recv_sem=x_recv.at[c, b, k],
                device_id={"snap": source},
                device_id_type=MESH,
            ).wait_recv()

    def input_product(b):
        count = 256 // BATCHES[b] if b == 0 else 4
        size = count * BATCHES[b]

        def some(i, _):
            rows = pl.ds(pl.multiple_of(i * size, size), size)
            steps = pl.ds(i * count, count)
            both = [xin[b][c, steps].reshape(size, LANES) for c in (0, 1)]
            pre[b][rows] = dot3(jnp.concatenate(both, axis=1), in_high[...], in_low[...]) + bias_ref[...]
            return 0

        lax.fori_loop(0, SNAPS // count, some, 0)

    def z_copy(b, s):
        return pltpu.make_async_remote_copy(
            src_ref=zout[b].at[s],
            dst_ref=shares(zin, slice(None), b, snap),
            send_sem=z_send.at[b, s],
            recv_sem=z_recv.at[b, snap],
            device_id={"snap": s},
            device_id_type=MESH,
        )

    def z_local(b):
        return pltpu.make_async_copy(zout[b].at[snap], shares(zin, slice(None), b, snap), local_sem.at[b])

    def z_start(b, s, z):
        zout[b][s, 0] = z[:, :LANES]
        zout[b][s, 1] = z[:, LANES:]

        @pl.when(s != snap)
        def _():
            z_copy(b, s).start()

        @pl.when(s == snap)
        def _():
            z_local(b).start()

    def z_wait(b):
        z_local(b).wait()
        for source in others:
            pltpu.make_async_remote_copy(
                src_ref=shares(zin, slice(None), b, source),
                dst_ref=shares(zin, slice(None), b, source),
                send_sem=z_send.at[b, source],
                recv_sem=z_recv.at[b, source],
                device_id={"snap": source},
                device_id_type=MESH,
            ).wait_recv()
        for c in (0, 1):
            size = SNAPS * BATCHES[b]
            own = pl.ds(me * BLOCKS + firsts[b] // EDGE, size // EDGE)
            bufs[c][own] = zin[c, firsts[b] : firsts[b] + size].reshape(size // EDGE, EDGE, LANES)

    def cell(gates, state_c):
        i, f, g, o = (gates[:, q * HIDDEN : (q + 1) * HIDDEN] for q in range(4))
        state_c = sigmoid(f) * state_c + sigmoid(i) * jnp.tanh(g)
        return sigmoid(o) * jnp.tanh(state_c), state_c

    def begin(b):
        return cell(pre[b][: BATCHES[b]], jnp.zeros((BATCHES[b], HIDDEN), F32))

    def product(h):
        high, low = halves(h)
        both = dot(jnp.concatenate([high, low], axis=0), rec_high[...])
        rows = h.shape[0]
        return both[:rows] + (both[rows:] + dot(high, rec_low[...]))

    def steps(b, start, stop, carry):
        def advance(s, carry):
            h, state_c = carry
            wide = product(h)
            rows = pl.ds(pl.multiple_of(s * BATCHES[b], 16), BATCHES[b])
            new = cell(pre[b][rows] + wide[:, : 4 * HIDDEN], state_c)
            z_start(b, s - 1, wide[:, 4 * HIDDEN :])
            return new

        return lax.fori_loop(start, stop, advance, carry)

    def finish(b, carry):
        last = slice(4 * HIDDEN, 5 * HIDDEN)
        z_start(b, SNAPS - 1, dot3(carry[0], rec_high[:, last], rec_low[:, last]))

    split_tiles(0, 4)
    one[0].ring()
    split_tiles(4, 8)
    for copy in weights:
        copy.wait()
    in_high[...], in_low[...] = halves(w_in[...])
    rec_high[:, : 4 * HIDDEN], rec_low[:, : 4 * HIDDEN] = halves(w_rec[...])
    rec_high[:, 4 * HIDDEN :], rec_low[:, 4 * HIDDEN :] = halves(w_two[...])
    one[0].onward(0)
    one[0].opposite()
    one[1].own()
    one[0].onward(-1)
    one[0].onward(1)
    one[1].ring()
    one[0].onward(2)
    one[1].onward(0)
    one[1].opposite()
    one[0].last()

    conv(0, 0, EARLY, True)
    x_start(0, 0)
    conv(0, EARLY, 4, True)
    one[1].onward(-1)
    one[1].onward(1)
    conv(0, 4, BLOCKS, True)
    x_start(0, 1)
    one[1].onward(2)
    x_wait(0, 0)
    x_wait(0, 1)
    one[1].last()

    conv(1, 0, EARLY, True)
    x_start(1, 0)
    conv(1, EARLY, BLOCKS, True)
    x_start(1, 1)

    x_wait(1, 0)
    input_product(0)
    finish(0, steps(0, 1, SNAPS, begin(0)))
    one[0].wait_sent()
    one[1].wait_sent()
    for device in beside:
        pl.semaphore_signal(free_sem, inc=1, device_id={"vtx": device}, device_id_type=MESH)
    x_wait(1, 1)
    input_product(1)
    z_wait(0)
    pl.semaphore_wait(free_sem, len(beside))
    two = [
        [
            Gather(bufs[c], first, count, g_send, g_recv, (2 + 2 * b + c) * GATHER_SEMS)
            for c in (0, 1)
        ]
        for b, (first, count) in enumerate(((0, EARLY), (EARLY, BLOCKS - EARLY)))
    ]
    two[0][0].own()
    two[0][1].own()
    finish(1, steps(1, 1, SNAPS, begin(1)))
    two[0][0].ring()
    two[0][1].ring()
    two[0][0].onward(0)
    two[0][0].opposite()
    two[0][1].onward(0)
    two[0][1].opposite()
    for da in (-1, 1, 2):
        two[0][0].onward(da)
        two[0][1].onward(da)
    z_wait(1)
    two[1][0].own()
    two[1][1].own()
    two[0][0].last()
    two[0][1].last()
    two[1][0].ring()
    two[1][0].onward(0)
    two[1][0].opposite()
    two[1][1].ring()
    two[1][0].onward(-1)
    two[1][0].onward(1)
    two[1][1].onward(0)
    two[1][1].opposite()
    two[1][0].onward(2)
    two[1][0].last()
    conv(0, 0, 4, False)
    two[1][1].onward(-1)
    two[1][1].onward(1)
    conv(0, 4, 8, False)
    two[1][1].onward(2)
    two[1][1].last()
    conv(1, 0, 8, False)

    for b in (0, 1):
        for c in (0, 1):
            two[b][c].wait_sent()
    for copy in x_sent:
        copy.wait_send()
    for b in (0, 1):
        for device in others:
            z_copy(b, device).wait_send()


def on_device(feats, col_ids, tiles, w_first, w_input, w_recur, lstm_bias, w_second):
    everyone = (lax.axis_size("vtx") * BLOCKS, EDGE, LANES)
    vmem, hbm = pl.BlockSpec(memory_space=pltpu.VMEM), pl.BlockSpec(memory_space=pl.ANY)
    dma = pltpu.SemaphoreType.DMA
    out = pl.pallas_call(
        kernel,
        in_specs=[pl.BlockSpec(memory_space=pltpu.SMEM), vmem, *[hbm] * 6],
        out_specs=vmem,
        out_shape=pltpu.VMEM((ROWS, HIDDEN), F32),
        scratch_shapes=[
            pltpu.VMEM(everyone, F32),
            pltpu.VMEM(everyone, F32),
            pltpu.VMEM((BLOCKS, KT, EDGE, EDGE), F32),
            pltpu.VMEM((BLOCKS, 2 * EDGE, KT * EDGE), BF16),
            pltpu.VMEM((BLOCKS, EDGE, LANES), F32),
            pltpu.VMEM((2, KT * EDGE, 2 * LANES), BF16),
            pltpu.VMEM((2, ROWS, LANES), F32),
            *[pltpu.VMEM((2, SNAPS, batch, LANES), F32) for batch in BATCHES],
            *[pltpu.VMEM((SNAPS * batch, 4 * HIDDEN), F32) for batch in BATCHES],
            *[pltpu.VMEM((SNAPS, 2, batch, LANES), F32) for batch in BATCHES],
            pltpu.VMEM((2, ROWS, LANES), F32),
            pltpu.VMEM(feats.shape[1:], F32),
            pltpu.VMEM(w_first.shape, F32),
            pltpu.VMEM((HIDDEN, 4 * HIDDEN), F32),
            pltpu.VMEM((HIDDEN, 4 * HIDDEN), F32),
            pltpu.VMEM((HIDDEN, HIDDEN), F32),
            pltpu.VMEM((HIDDEN, 4 * HIDDEN), BF16),
            pltpu.VMEM((HIDDEN, 4 * HIDDEN), BF16),
            pltpu.VMEM((HIDDEN, 5 * HIDDEN), BF16),
            pltpu.VMEM((HIDDEN, 5 * HIDDEN), BF16),
            dma((6 * GATHER_SEMS,)),
            dma((6 * GATHER_SEMS,)),
            dma((2, 2, SNAPS)),
            dma((2, 2, SNAPS)),
            dma((2, SNAPS)),
            dma((2, SNAPS)),
            dma((2,)),
            dma((BLOCKS,)),
            dma((BLOCKS + 2,)),
            dma((3,)),
            pltpu.SemaphoreType.REGULAR,
        ],
        compiler_params=pltpu.CompilerParams(
            collective_id=0, has_side_effects=True, vmem_limit_bytes=56 << 20
        ),
    )(
        col_ids[0], lstm_bias.reshape(1, -1), feats[0], w_first, tiles[0], w_input, w_recur, w_second
    )
    return out[None]


def solution(mesh):
    placed = (
        P("snap", "vtx", None),
        P("snap", "vtx", None),
        P("snap", "vtx", None, None, None),
        P(),
        P(),
        P(),
        P(),
        P(),
    )
    return jax.shard_map(
        on_device, mesh=mesh, in_specs=placed, out_specs=P("snap", "vtx", None), check_vma=False
    )
```
